256 devices in a mesh: pat: 16 (over z, core), pb: 16 (over x, y).
Axes of the slice: x: 4, y: 4, z: 8, core: 2. Of those that a mesh axis runs over, the one named last changes fastest.
Arguments:
- measured: float32 [32768, 4096], P(('pat', 'pb')), may hold values from 1 to 10
- resolution: float32 [33, 4096], replicated, may hold values from 0.05 to 1
- loadings_start: float32 [32768, 128], P('pat'), may hold values from 0.05 to 0.5
- components_start: float32 [128, 4096], P(None, 'pb'), may hold values from 0.05 to 0.5
Outputs:
- loadings: float32 [32768, 128], P('pat')
- components: float32 [128, 4096], P(None, 'pb')
The draws below stay inside these ranges and needn't reach their ends.
All inputs are finite; a program needn't handle non-finite values.
Results may differ from the reference program's by a relative error of at most 0.00013.
Values sent between devices are 32-bit elements; how exact they have to be, the bound alone decides.
No kernel may reach another device: no remote copies, remote signals or barrier semaphores. Data moves between devices by JAX's collectives and lax.ppermute only.
A program may use at most 128 MiB of HBM per device.

```python
import math
import jax
import jax.numpy as jnp
from jax import lax

Q = 4096
COMPONENTS = 128
RADIUS = 16
TAPS = 33
ITERS = 3
PATTERNS = 32768


def steps_of(own_key, dims, split, least, high):
    def one(position, parts):
        heights = jax.random.uniform(jax.random.fold_in(jax.random.fold_in(own_key, 6), position), (parts,), jnp.float32, least / len(split), high / len(split))
        return jnp.repeat(jnp.exp(heights), dims[position] // parts).reshape((-1,) + (1,) * (len(dims) - position - 1))

    loudness = one(*split[0])
    for cut in split[1:]:
        loudness = loudness * one(*cut)
    return loudness


def setup_inputs(seed: int = 0) -> dict:
    arg_keys = jax.random.split(jax.random.key(seed), 5)
    return {
        "measured": jnp.clip(jnp.exp(math.log(10.0) - 2.3025851 * jax.random.uniform(arg_keys[0], (PATTERNS, Q), jnp.float32) ** steps_of(arg_keys[0], (PATTERNS, Q), ((0, 256),), -0.2, 0.2)), 1.0, 10.0),
        "resolution": jnp.clip(jnp.exp(jax.random.uniform(arg_keys[1], (TAPS, Q), jnp.float32, math.log(0.05), math.log(1.0))), 0.05, 1.0),
        "loadings_start": jnp.clip(jnp.exp(math.log(0.5) - 2.3025851 * jax.random.uniform(arg_keys[2], (PATTERNS, COMPONENTS), jnp.float32) ** steps_of(arg_keys[2], (PATTERNS, COMPONENTS), ((0, 16),), -0.2, 0.2)), 0.05, 0.5),
        "components_start": jnp.clip(jnp.exp(math.log(0.5) - 2.3025851 * jax.random.uniform(arg_keys[3], (COMPONENTS, Q), jnp.float32) ** steps_of(arg_keys[3], (COMPONENTS, Q), ((1, 16),), -0.2, 0.2)), 0.05, 0.5),
    }


def smear_forward(field, resolution):
    width = field.shape[1]
    padded = jnp.pad(field, ((0, 0), (RADIUS, RADIUS)))
    total = jnp.zeros(field.shape, jnp.float32)
    for offset in range(2 * RADIUS + 1):
        total = total + resolution[offset][None, :] * padded[:, offset:offset + width]
    return total


def smear_back(field, resolution):
    width = field.shape[1]
    total = jnp.zeros(field.shape, jnp.float32)
    for offset in range(2 * RADIUS + 1):
        weighted = jnp.pad(resolution[offset][None, :] * field, ((0, 0), (RADIUS, RADIUS)))
        begin = 2 * RADIUS - offset
        total = total + weighted[:, begin:begin + width]
    return total


def correct_block(measured, resolution):
    blurred = smear_forward(measured, resolution)
    back = smear_back(measured / blurred, resolution)
    weight_sum = smear_back(jnp.ones((1, measured.shape[1]), jnp.float32), resolution)
    return measured * back / weight_sum


def reference(measured, resolution, loadings_start, components_start):
    rows = measured.shape[0]
    block = min(rows, 1024)
    stacked = measured.reshape(rows // block, block, measured.shape[1])
    corrected = lax.map(lambda piece: correct_block(piece, resolution), stacked).reshape(measured.shape)
    loadings = loadings_start
    components = components_start
    high = lax.Precision.HIGHEST
    for step in range(ITERS):
        quotient = corrected / jnp.dot(loadings, components, precision=high)
        numerator = jnp.dot(loadings.T, quotient, precision=high)
        w_totals = jnp.sum(loadings, axis=0)
        components = components * numerator / w_totals[:, None]
        quotient = corrected / jnp.dot(loadings, components, precision=high)
        numerator = jnp.dot(quotient, components.T, precision=high)
        h_totals = jnp.sum(components, axis=1)
        loadings = loadings * numerator / h_totals[None, :]
    return loadings, components
```

```python
import functools
import jax
import jax.numpy as jnp
from jax import lax
from jax.experimental import pallas as pl
from jax.experimental.pallas import tpu as pltpu
from jax.sharding import Mesh, PartitionSpec as P

RADIUS = 16
TAPS = 33
ITERS = 3
LANES = 128
VMEM = pltpu.MemorySpace.VMEM
SMEM = pltpu.MemorySpace.SMEM
F32 = jnp.float32
BF16 = jnp.bfloat16


def split(x):
    hi = x.astype(BF16)
    return hi, (x - hi.astype(F32)).astype(BF16)


def mm(a, b, dims):
    return lax.dot_general(a, b, (dims, ((), ())), preferred_element_type=F32)


def mm3(a, b, dims):
    (ah, al), (bh, bl) = a, b
    return mm(ah, bh, dims) + (mm(al, bh, dims) + mm(ah, bl, dims))


NT = ((1,), (1,))
NN = ((1,), (0,))


def smear_kernel(blocks, idx_ref, field_ref, res_ref, o0, o1, o2, o3, vh, vl, uh, ul, ch, cl, hh, hl, pad):
    rows = field_ref.shape[0]
    xi, ci = idx_ref[0], idx_ref[1]
    zero = jnp.zeros((rows, LANES), BF16)
    for ref in (vh, vl, uh, ul):
        ref[:, 0:LANES] = zero
        ref[:, (blocks + 1) * LANES : (blocks + 2) * LANES] = zero
    zero = jnp.zeros((LANES, LANES), BF16)
    for ref in (ch, cl, hh, hl):
        ref[0:LANES, :] = zero
        ref[(blocks + 1) * LANES : (blocks + 2) * LANES, :] = zero
    pad[...] = jnp.zeros((LANES, LANES), F32)
    near = lax.broadcasted_iota(jnp.int32, (rows, LANES), 1) < LANES // 2
    row = lax.broadcasted_iota(jnp.int32, (LANES, LANES), 0)
    col = lax.broadcasted_iota(jnp.int32, (LANES, LANES), 1)
    inside = jnp.abs(row - col) <= RADIUS

    def at(j):
        return pl.ds(pl.multiple_of((j + 1) * LANES, LANES), LANES)

    def window(ref, j):
        halo = jnp.where(near, ref[:, at(j + 1)], ref[:, at(j - 1)])
        return jnp.concatenate([ref[:, at(j)], halo], axis=1)

    def prepare(j, _):
        cols = pl.ds(pl.multiple_of(j * LANES, LANES), LANES)
        h, l = split(field_ref[:, cols])
        vh[:, at(j)] = h
        vl[:, at(j)] = l
        pad[0:TAPS, :] = res_ref[:, cols]
        band = pltpu.roll(jnp.transpose(pad[...]), LANES - RADIUS, 1, stride=1, stride_axis=0)
        h, l = split(jnp.where(inside, band, 0.0))
        ch[at(j), :] = h
        cl[at(j), :] = l
        h, l = split(jnp.where(inside, 0.0, band))
        hh[at(j), :] = h
        hl[at(j), :] = l
        return _

    lax.fori_loop(0, blocks, prepare, 0, unroll=2)

    def forward(j, _):
        cols = pl.ds(pl.multiple_of(j * LANES, LANES), LANES)
        bh = jnp.concatenate([ch[at(j), :], hh[at(j), :]], axis=1)
        bl = jnp.concatenate([cl[at(j), :], hl[at(j), :]], axis=1)
        blurred = mm3((window(vh, j), window(vl, j)), (bh, bl), NT)
        h, l = split(field_ref[:, cols] / blurred)
        uh[:, at(j)] = h
        ul[:, at(j)] = l
        return _

    lax.fori_loop(0, blocks, forward, 0, unroll=4)

    def stack(c, h, j):
        half = LANES // 2
        after = h[pl.ds(pl.multiple_of((j + 2) * LANES, LANES), half), :]
        before = h[pl.ds(pl.multiple_of(j * LANES + half, half), half), :]
        return jnp.concatenate([c[at(j), :], after, before], axis=0)

    per = blocks // 4
    for d, out in enumerate((o0, o1, o2, o3)):
        def back(i, _):
            j = (xi ^ d) * per + (i ^ (ci * (per // 2)))
            bh = stack(ch, hh, j)
            bl = stack(cl, hl, j)
            total = mm3((window(uh, j), window(ul, j)), (bh, bl), NN)
            weight = jnp.sum(bh.astype(F32) + bl.astype(F32), axis=0, keepdims=True)
            v = field_ref[:, pl.ds(pl.multiple_of(j * LANES, LANES), LANES)]
            out[:, pl.ds(pl.multiple_of(i * LANES, LANES), LANES)] = v * total / weight
            return _

        lax.fori_loop(0, per, back, 0, unroll=4)


def whole(n, space=VMEM):
    return [pl.BlockSpec(memory_space=space)] * n


def smear(idx, field, resolution):
    rows, width = field.shape
    blocks = width // LANES
    padded = (blocks + 2) * LANES
    return pl.pallas_call(
        functools.partial(smear_kernel, blocks),
        out_shape=[jax.ShapeDtypeStruct((rows, width // 4), F32)] * 4,
        in_specs=whole(1, SMEM) + whole(2),
        out_specs=whole(4),
        scratch_shapes=[pltpu.VMEM((rows, padded), BF16)] * 4
        + [pltpu.VMEM((padded, LANES), BF16)] * 4
        + [pltpu.VMEM((LANES, LANES), F32)],
        compiler_params=pltpu.CompilerParams(vmem_limit_bytes=48 << 20),
        name="smear",
    )(idx, field, resolution)


def fold(x):
    return jnp.sum(x.reshape(x.shape[0] // 8, 8, x.shape[1]), axis=0)


def components_kernel(x0, x1, x2, x3, l0, l1, l2, l3, ha, hb, keep, send):
    loads = jnp.concatenate([l0[...], l1[...], l2[...], l3[...]], axis=0)
    pair = split(loads)
    pair_t = split(jnp.transpose(loads))
    sums = fold(loads)
    half = ha.shape[0]
    tile = 256
    for h_ref, out, base in ((hb, send, half), (ha, keep, 0)):
        for t in range(half // tile):
            h = split(h_ref[t * tile : (t + 1) * tile, :])
            cols = slice(base + t * tile, base + (t + 1) * tile)
            x = jnp.concatenate([r[:, cols] for r in (x0, x1, x2, x3)], axis=0)
            quotient = split(x / mm3(pair, h, NT))
            out[t * tile : (t + 1) * tile, :] = jnp.transpose(mm3(pair_t, quotient, NN))
        out[half : half + 8, :] = sums


def components_part(xs, ls, ha, hb):
    half, comps = ha.shape
    return pl.pallas_call(
        components_kernel,
        out_shape=[jax.ShapeDtypeStruct((half + 8, comps), F32)] * 2,
        in_specs=whole(10),
        out_specs=whole(2),
        compiler_params=pltpu.CompilerParams(vmem_limit_bytes=48 << 20),
        name="components_part",
    )(*xs, *ls, ha, hb)


def loadings_kernel(x0, x1, x2, x3, l0, l1, l2, l3, ha, hb, o0, o1, o2, o3):
    h = jnp.concatenate([ha[...], hb[...]], axis=0)
    pair = split(h)
    sums = fold(h)
    for x, l, out in zip((x0, x1, x2, x3), (l0, l1, l2, l3), (o0, o1, o2, o3)):
        rows = x.shape[0]
        quotient = split(x[...] / mm3(split(l[...]), pair, NT))
        out[0:rows, :] = mm3(quotient, pair, NN)
        out[rows : rows + 8, :] = sums


def loadings_part(xs, ls, ha, hb):
    rows, comps = ls[0].shape
    return pl.pallas_call(
        loadings_kernel,
        out_shape=[jax.ShapeDtypeStruct((rows + 8, comps), F32)] * 4,
        in_specs=whole(10),
        out_specs=whole(4),
        compiler_params=pltpu.CompilerParams(vmem_limit_bytes=48 << 20),
        name="loadings_part",
    )(*xs, *ls, ha, hb)


SPLIT = ("z", "c", "x", "y")


def swap(x, axis, distance):
    size = 2 if axis == "c" else 4
    return lax.ppermute(x, axis, [(i, i ^ distance) for i in range(size)])


def spread(x, axes, copies):
    y = jnp.broadcast_to(x[None], (copies,) + x.shape)
    return lax.all_to_all(y, axes, 0, 0).reshape((-1,) + x.shape[1:])


def local(measured, resolution, loadings_start, components_start):
    xi, yi, ci = lax.axis_index("x"), lax.axis_index("y"), lax.axis_index("c")
    zi = lax.axis_index("z")
    comps = components_start.shape[0]
    start = spread(components_start.T, "y", 4)
    half = start.shape[0] // 2
    mine = lax.dynamic_slice_in_dim(start, ci * half, half)
    theirs = lax.dynamic_slice_in_dim(start, (1 - ci) * half, half)
    idx = jnp.stack([xi, ci]).astype(jnp.int32)
    chunks = smear(idx, measured, resolution)
    xs = [chunks[0]] + [swap(chunks[d], "x", d) for d in (1, 2, 3)]
    rows = measured.shape[0]
    ls = [lax.dynamic_slice_in_dim(loadings_start, ((xi ^ d) * 4 + yi) * rows, rows) for d in range(4)]
    group = 32
    part = half // group
    piece = lax.dynamic_slice_in_dim(mine, (zi * 4 + yi) * part, part)
    for step in range(ITERS):
        keep, send = components_part(xs, ls, mine, theirs)
        both = keep + swap(send, "c", 1)
        packed = jnp.concatenate(
            [both[:half].reshape(group, part, comps), jnp.broadcast_to(both[half:][None], (group, 8, comps))], axis=1
        )
        total = jnp.sum(lax.all_to_all(packed, ("z", "y"), 0, 0), axis=0)
        piece = piece * total[:part] / jnp.sum(total[part:], axis=0, keepdims=True)
        mine = spread(piece, ("z", "y"), group)
        theirs = swap(mine, "c", 1)
        parts = loadings_part(xs, ls, mine, theirs)
        total = parts[0] + swap(parts[1], "x", 1) + swap(parts[2], "x", 2) + swap(parts[3], "x", 3)
        own = ls[0] * total[:rows] / jnp.sum(total[rows:], axis=0, keepdims=True)
        if step < ITERS - 1:
            ls = [own] + [swap(own, "x", d) for d in (1, 2, 3)]
    loadings = spread(own, ("x", "y"), 16)
    low = lax.dynamic_slice_in_dim(mine, (yi % 2) * (half // 2), half // 2)
    high = lax.dynamic_slice_in_dim(theirs, (yi % 2) * (half // 2), half // 2)
    components = jnp.where(yi // 2 == ci, low, high).T
    return (loadings, components)


def solution(mesh):
    inner = Mesh(mesh.devices.reshape(8, 2, 4, 4), SPLIT)
    return jax.shard_map(
        local,
        mesh=inner,
        in_specs=(P(SPLIT, None), P(), P(("z", "c"), None), P(None, ("x", "y"))),
        out_specs=(P(("z", "c"), None), P(None, ("x", "y"))),
        check_vma=False,
    )
```

```python
import functools
import jax
import jax.numpy as jnp
from jax import lax
from jax.experimental import pallas as pl
from jax.experimental.pallas import tpu as pltpu
from jax.sharding import Mesh, PartitionSpec as P

RADIUS = 16
TAPS = 33
ITERS = 3
LANES = 128
VMEM = pltpu.MemorySpace.VMEM
SMEM = pltpu.MemorySpace.SMEM
F32 = jnp.float32
BF16 = jnp.bfloat16
NT = ((1,), (1,))
NN = ((1,), (0,))


def split(x):
    hi = x.astype(BF16)
    return hi, (x - hi.astype(F32)).astype(BF16)


def mm(a, b, dims):
    return lax.dot_general(a, b, (dims, ((), ())), preferred_element_type=F32)


def mm3(a, b, dims):
    (ah, al), (bh, bl) = a, b
    return mm(ah, bh, dims) + (mm(al, bh, dims) + mm(ah, bl, dims))


def mm_short(a, b, dims):
    (ah, al), (bh, bl) = a, b
    axis = dims[1][0]
    wide = mm(jnp.concatenate([ah, al], axis=1), jnp.concatenate([bh, bh], axis=axis), dims)
    return wide + mm(ah, bl, dims)


def block(j):
    return pl.ds(pl.multiple_of(j * LANES, LANES), LANES)


def call(kernel, outs, ins, name, macs, scratch=(), scalars=0, aliases=None):
    cost = 1024 if name == "smear" else 1 << 20
    kept = [jax.ShapeDtypeStruct(ins[i].shape, ins[i].dtype) for i in (aliases or {})]
    result = pl.pallas_call(
        kernel,
        out_shape=[jax.ShapeDtypeStruct(o, F32) for o in outs] + kept,
        in_specs=[pl.BlockSpec(memory_space=SMEM)] * scalars + [pl.BlockSpec(memory_space=VMEM)] * (len(ins) - scalars),
        out_specs=[pl.BlockSpec(memory_space=VMEM)] * (len(outs) + len(kept)),
        scratch_shapes=list(scratch),
        input_output_aliases=aliases or {},
        compiler_params=pltpu.CompilerParams(vmem_limit_bytes=16 << 20),
        cost_estimate=pl.CostEstimate(flops=cost, bytes_accessed=cost, transcendentals=0),
        name=name,
    )(*ins)
    return result


def bands_kernel(blocks, res_ref, bh, bl, pad):
    zero = jnp.zeros((LANES, 2 * LANES), BF16)
    for ref in (bh, bl):
        ref[0:LANES, :] = zero
        ref[(blocks + 1) * LANES : (blocks + 2) * LANES, :] = zero
    for ref in pad:
        ref[...] = jnp.zeros((LANES, LANES), F32)
    row = lax.broadcasted_iota(jnp.int32, (LANES, LANES), 0)
    col = lax.broadcasted_iota(jnp.int32, (LANES, LANES), 1)
    inside = jnp.abs(row - col) <= RADIUS

    def one(j, ref):
        ref[0:TAPS, :] = res_ref[:, block(j)]
        band = pltpu.roll(jnp.transpose(ref[...]), LANES - RADIUS, 1, stride=1, stride_axis=0)
        h, l = split(jnp.where(inside, band, 0.0))
        bh[block(j + 1), 0:LANES] = h
        bl[block(j + 1), 0:LANES] = l
        h, l = split(jnp.where(inside, 0.0, band))
        bh[block(j + 1), LANES:] = h
        bl[block(j + 1), LANES:] = l

    def step(i, carry):
        for u, ref in enumerate(pad):
            one(i * len(pad) + u, ref)
        return carry

    lax.fori_loop(0, blocks // len(pad), step, 0)


def make_bands(resolution):
    blocks = resolution.shape[1] // LANES
    shape = jax.ShapeDtypeStruct(((blocks + 2) * LANES, 2 * LANES), BF16)

    def kernel(res_ref, bh, bl, p0, p1, p2, p3):
        bands_kernel(blocks, res_ref, bh, bl, (p0, p1, p2, p3))

    return pl.pallas_call(
        kernel,
        out_shape=[shape] * 2,
        in_specs=[pl.BlockSpec(memory_space=VMEM)],
        out_specs=[pl.BlockSpec(memory_space=VMEM)] * 2,
        scratch_shapes=[pltpu.VMEM((LANES, LANES), F32)] * 4,
        compiler_params=pltpu.CompilerParams(vmem_limit_bytes=16 << 20),
        cost_estimate=pl.CostEstimate(flops=1 << 20, bytes_accessed=12 << 20, transcendentals=0),
        name="bands",
    )(resolution)


def smear_kernel(blocks, d, idx_ref, field_ref, bh_ref, bl_ref, out, token, _, __, ___, vh, vl, uh, ul):
    token[...] = jnp.zeros(token.shape, F32)
    rows = field_ref.shape[0]
    per = blocks // 4
    base = (idx_ref[0] ^ d) * per
    flip = idx_ref[1] * (per // 2)
    near = lax.broadcasted_iota(jnp.int32, (rows, LANES), 1) < LANES // 2

    def field(j):
        return field_ref[:, block(jnp.clip(j, 0, blocks - 1))]

    def at(i):
        return slice(i * LANES, (i + 1) * LANES)

    def window(ref, i):
        return jnp.concatenate([ref[:, at(i)], jnp.where(near, ref[:, at(i + 1)], ref[:, at(i - 1)])], axis=1)

    for i in range(per + 4):
        v = field(base + i - 2)
        if i < 2:
            v = jnp.where(base > 0, v, 0.0)
        if i >= per + 2:
            v = jnp.where(base + per < blocks, v, 0.0)
        vh[:, at(i)], vl[:, at(i)] = split(v)
    for i in range(per + 2):
        band = block(base + i)
        blurred = mm3((window(vh, i + 1), window(vl, i + 1)), (bh_ref[band, :], bl_ref[band, :]), NT)
        u = field(base + i - 1) / blurred
        if i < 1:
            u = jnp.where(base > 0, u, 0.0)
        if i >= per + 1:
            u = jnp.where(base + per < blocks, u, 0.0)
        uh[:, at(i)], ul[:, at(i)] = split(u)

    def stack(ref, j):
        half = LANES // 2
        after = ref[pl.ds(pl.multiple_of((j + 1) * LANES, LANES), half), LANES:]
        before = ref[pl.ds(pl.multiple_of((j - 1) * LANES + half, half), half), LANES:]
        return jnp.concatenate([ref[block(j), 0:LANES], after, before], axis=0)

    for i in range(per):
        bh = stack(bh_ref, base + i + 1)
        bl = stack(bl_ref, base + i + 1)
        total = mm3((window(uh, i + 1), window(ul, i + 1)), (bh, bl), NN)
        weight = jnp.sum(bh.astype(F32) + bl.astype(F32), axis=0, keepdims=True)
        out[:, block(i ^ flip)] = field(base + i) * total / weight


def smear(d, idx, field, bh, bl):
    rows, width = field.shape
    blocks = width // LANES
    per = blocks // 4
    scratch = [pltpu.VMEM((rows, (per + 4) * LANES), BF16)] * 2 + [pltpu.VMEM((rows, (per + 2) * LANES), BF16)] * 2
    return call(
        functools.partial(smear_kernel, blocks, d),
        [(rows, width // 4), (8, LANES)],
        [idx, field, bh, bl],
        "smear",
        rows * width * LANES,
        scratch,
        1,
        {1: 2, 2: 3, 3: 4},
    )


def fold(x):
    return jnp.sum(jnp.sum(x.reshape(4, x.shape[0] // 32, 8, x.shape[1]), axis=1), axis=0)


def numerator(x, loads, pair, tile):
    return mm_short(split(jnp.transpose(loads)), split(x / mm_short(split(loads), pair, NT)), NN)


def first_kernel(l, h, x, out, sums):
    half = h.shape[0]
    out[...] = numerator(x[:, half:], l[...], split(h[...]), half)
    sums[...] = fold(l[...])


def middle_kernel(l, h, x, before, before_sums, out, sums):
    half = h.shape[0]
    out[...] = before[...] + numerator(x[:, half:], l[...], split(h[...]), half)
    sums[...] = before_sums[...] + fold(l[...])


def last_kernel(l, h, x, before, before_sums, out):
    half = h.shape[0]
    out[0:half, :] = jnp.transpose(before[...] + numerator(x[:, half:], l[...], split(h[...]), half))
    out[half : half + 8, :] = before_sums[...] + fold(l[...])


def keep_kernel(x0, x1, x2, x3, l0, l1, l2, l3, h_ref, out):
    half = h_ref.shape[0]
    loads = jnp.concatenate([l[...] for l in (l0, l1, l2, l3)], axis=0)
    left, left_t = split(loads), split(jnp.transpose(loads))
    tile = 256
    for t in range(half // tile):
        h = split(h_ref[t * tile : (t + 1) * tile, :])
        x = jnp.concatenate([r[:, t * tile : (t + 1) * tile] for r in (x0, x1, x2, x3)], axis=0)
        quotient = split(x / mm_short(left, h, NT))
        out[t * tile : (t + 1) * tile, :] = jnp.transpose(mm3(left_t, quotient, NN))
    out[half : half + 8, :] = fold(loads)


def components_part(xs, ls, mine, theirs, order):
    half, comps = mine.shape
    rows = xs[0].shape[0]
    macs = 2 * rows * half * comps
    a, b, c, d = order
    state = call(first_kernel, [(comps, half), (8, comps)], [ls[a], theirs, xs[a]], "components_first", macs)
    state = call(middle_kernel, [(comps, half), (8, comps)], [ls[b], theirs, xs[b], *state], "components_middle", macs)
    state = call(middle_kernel, [(comps, half), (8, comps)], [ls[c], theirs, xs[c], *state], "components_middle", macs)
    send = call(last_kernel, [(half + 8, comps)], [ls[d], theirs, xs[d], *state], "components_last", macs)[0]
    keep = call(keep_kernel, [(half + 8, comps)], [*xs, *ls, mine], "components_keep", 4 * macs)[0]
    return keep, send


def own_half_kernel(x0, x1, x2, x3, l0, l1, l2, l3, h_ref, o0, o1, o2, o3):
    pair = split(h_ref[...])
    half = h_ref.shape[0]
    for x, l, out in zip((x0, x1, x2, x3), (l0, l1, l2, l3), (o0, o1, o2, o3)):
        out[...] = mm3(split(x[:, 0:half] / mm_short(split(l[...]), pair, NT)), pair, NN)


def other_half_kernel(x, l, h_ref, own, before, out):
    pair = split(h_ref[...])
    half = h_ref.shape[0]
    rows = l.shape[0]
    out[0:rows, :] = before[...] + mm3(split(x[:, half:] / mm_short(split(l[...]), pair, NT)), pair, NN)
    out[rows : rows + 8, :] = fold(h_ref[...]) + fold(own[...])


def loadings_part(xs, ls, mine, theirs):
    half, comps = mine.shape
    rows = xs[0].shape[0]
    macs = 2 * rows * half * comps
    first = call(own_half_kernel, [(rows, comps)] * 4, [*xs, *ls, mine], "loadings_own", 4 * macs)
    return [
        call(other_half_kernel, [(rows + 8, comps)], [xs[d], ls[d], theirs, mine, first[d]], "loadings_other", macs)[0]
        for d in range(4)
    ]


SPLIT = ("z", "c", "x", "y")


def swap(x, axis, distance):
    size = 2 if axis == "c" else 4
    return lax.ppermute(x, axis, [(i, i ^ distance) for i in range(size)])


def spread(x, axes, copies):
    y = jnp.broadcast_to(x[None], (copies,) + x.shape)
    return lax.all_to_all(y, axes, 0, 0).reshape((-1,) + x.shape[1:])


def local(measured, resolution, loadings_start, components_start):
    xi, yi, ci = lax.axis_index("x"), lax.axis_index("y"), lax.axis_index("c")
    zi = lax.axis_index("z")
    comps = components_start.shape[0]
    idx = jnp.stack([xi, ci]).astype(jnp.int32)
    bh, bl = make_bands(resolution)
    field = measured
    xs = [None] * 4
    for d in (2, 1, 3, 0):
        xs[d], zero, field, bh, bl = smear(d, idx, field, bh, bl)
        if d:
            xs[d] = swap(xs[d], "x", d)
    start = spread((components_start + zero[0, 0]).T, "y", 4)
    half = start.shape[0] // 2
    mine = lax.dynamic_slice_in_dim(start, ci * half, half)
    theirs = lax.dynamic_slice_in_dim(start, (1 - ci) * half, half)
    rows = measured.shape[0]
    ls = [lax.dynamic_slice_in_dim(loadings_start, ((xi ^ d) * 4 + yi) * rows, rows) for d in range(4)]
    group = 32
    part = half // group
    piece = lax.dynamic_slice_in_dim(mine, (zi * 4 + yi) * part, part)
    for step in range(ITERS):
        keep, send = components_part(xs, ls, mine, theirs, (0, 1, 3, 2) if step else (0, 2, 1, 3))
        both = keep + swap(send, "c", 1)
        totals = jnp.sum(both[half:], axis=0)
        packed = jnp.concatenate(
            [both[:half].reshape(group, part, 1, comps), jnp.broadcast_to(totals, (group, 1, 1, comps))], axis=1
        )
        total = jnp.sum(lax.all_to_all(packed, ("z", "y"), 0, 0), axis=0)[:, 0]
        piece = piece * total[:part] / total[part:]
        mine = spread(piece, ("z", "y"), group)
        theirs = swap(mine, "c", 1)
        parts = loadings_part(xs, ls, mine, theirs)
        total = parts[0] + swap(parts[2], "x", 2) + swap(parts[1], "x", 1) + swap(parts[3], "x", 3)
        own = ls[0] * total[:rows] / jnp.sum(total[rows:], axis=0, keepdims=True)
        if step < ITERS - 1:
            ls = [own] + [swap(own, "x", d) for d in (1, 2, 3)]
    loadings = spread(own, ("x", "y"), 16)
    low = lax.dynamic_slice_in_dim(mine, (yi % 2) * (half // 2), half // 2)
    high = lax.dynamic_slice_in_dim(theirs, (yi % 2) * (half // 2), half // 2)
    components = jnp.where(yi // 2 == ci, low, high).T
    return (loadings, components)


def solution(mesh):
    inner = Mesh(mesh.devices.reshape(8, 2, 4, 4), SPLIT)
    return jax.shard_map(
        local,
        mesh=inner,
        in_specs=(P(SPLIT, None), P(), P(("z", "c"), None), P(None, ("x", "y"))),
        out_specs=(P(("z", "c"), None), P(None, ("x", "y"))),
        check_vma=False,
    )
```

```python
import functools
import jax
import jax.numpy as jnp
from jax import lax
from jax.experimental import pallas as pl
from jax.experimental.pallas import tpu as pltpu
from jax.sharding import Mesh, PartitionSpec as P

RADIUS = 16
TAPS = 33
ITERS = 3
LANES = 128
VMEM = pltpu.MemorySpace.VMEM
SMEM = pltpu.MemorySpace.SMEM
F32 = jnp.float32
BF16 = jnp.bfloat16
NT = ((1,), (1,))
NN = ((1,), (0,))


def split(x):
    hi = x.astype(BF16)
    return hi, (x - hi.astype(F32)).astype(BF16)


def mm(a, b, dims):
    return lax.dot_general(a, b, (dims, ((), ())), preferred_element_type=F32)


def mm3(a, b, dims):
    (ah, al), (bh, bl) = a, b
    return mm(ah, bh, dims) + (mm(al, bh, dims) + mm(ah, bl, dims))


def mm_short(a, b, dims):
    (ah, al), (bh, bl) = a, b
    axis = dims[1][0]
    wide = mm(jnp.concatenate([ah, al], axis=1), jnp.concatenate([bh, bh], axis=axis), dims)
    return wide + mm(ah, bl, dims)


def block(j):
    return pl.ds(pl.multiple_of(j * LANES, LANES), LANES)


def call(kernel, outs, ins, name, macs, scratch=(), scalars=0, aliases=None):
    cost = 1024 if name == "smear" else 1 << 20
    kept = [jax.ShapeDtypeStruct(ins[i].shape, ins[i].dtype) for i in (aliases or {})]
    result = pl.pallas_call(
        kernel,
        out_shape=[jax.ShapeDtypeStruct(o, F32) for o in outs] + kept,
        in_specs=[pl.BlockSpec(memory_space=SMEM)] * scalars + [pl.BlockSpec(memory_space=VMEM)] * (len(ins) - scalars),
        out_specs=[pl.BlockSpec(memory_space=VMEM)] * (len(outs) + len(kept)),
        scratch_shapes=list(scratch),
        input_output_aliases=aliases or {},
        compiler_params=pltpu.CompilerParams(vmem_limit_bytes=8 << 20),
        cost_estimate=pl.CostEstimate(flops=cost, bytes_accessed=cost, transcendentals=0),
        name=name,
    )(*ins)
    return result


def bands_kernel(blocks, res_ref, bh, bl, pad):
    zero = jnp.zeros((LANES, 2 * LANES), BF16)
    for ref in (bh, bl):
        ref[0:LANES, :] = zero
        ref[(blocks + 1) * LANES : (blocks + 2) * LANES, :] = zero
    for ref in pad:
        ref[...] = jnp.zeros((LANES, LANES), F32)
    row = lax.broadcasted_iota(jnp.int32, (LANES, LANES), 0)
    col = lax.broadcasted_iota(jnp.int32, (LANES, LANES), 1)
    inside = jnp.abs(row - col) <= RADIUS

    def one(j, ref):
        ref[0:TAPS, :] = res_ref[:, block(j)]
        band = pltpu.roll(jnp.transpose(ref[...]), LANES - RADIUS, 1, stride=1, stride_axis=0)
        h, l = split(jnp.where(inside, band, 0.0))
        bh[block(j + 1), 0:LANES] = h
        bl[block(j + 1), 0:LANES] = l
        h, l = split(jnp.where(inside, 0.0, band))
        bh[block(j + 1), LANES:] = h
        bl[block(j + 1), LANES:] = l

    def step(i, carry):
        for u, ref in enumerate(pad):
            one(i * len(pad) + u, ref)
        return carry

    lax.fori_loop(0, blocks // len(pad), step, 0)


def make_bands(resolution):
    blocks = resolution.shape[1] // LANES
    shape = jax.ShapeDtypeStruct(((blocks + 2) * LANES, 2 * LANES), BF16)

    def kernel(res_ref, bh, bl, p0, p1, p2, p3):
        bands_kernel(blocks, res_ref, bh, bl, (p0, p1, p2, p3))

    return pl.pallas_call(
        kernel,
        out_shape=[shape] * 2,
        in_specs=[pl.BlockSpec(memory_space=VMEM)],
        out_specs=[pl.BlockSpec(memory_space=VMEM)] * 2,
        scratch_shapes=[pltpu.VMEM((LANES, LANES), F32)] * 4,
        compiler_params=pltpu.CompilerParams(vmem_limit_bytes=8 << 20),
        cost_estimate=pl.CostEstimate(flops=1 << 20, bytes_accessed=12 << 20, transcendentals=0),
        name="bands",
    )(resolution)


def smear_kernel(blocks, d, idx_ref, field_ref, bh_ref, bl_ref, out, token, _, __, vh, vl, uh, ul):
    token[...] = jnp.zeros(token.shape, F32)
    rows = field_ref.shape[0]
    per = blocks // 4
    base = (idx_ref[0] ^ d) * per
    flip = idx_ref[1] * (per // 2)
    near = lax.broadcasted_iota(jnp.int32, (rows, LANES), 1) < LANES // 2

    def field(j):
        return field_ref[:, block(jnp.clip(j, 0, blocks - 1))]

    def at(i):
        return slice(i * LANES, (i + 1) * LANES)

    def window(ref, i):
        return jnp.concatenate([ref[:, at(i)], jnp.where(near, ref[:, at(i + 1)], ref[:, at(i - 1)])], axis=1)

    for i in range(per + 4):
        v = field(base + i - 2)
        if i < 2:
            v = jnp.where(base > 0, v, 0.0)
        if i >= per + 2:
            v = jnp.where(base + per < blocks, v, 0.0)
        vh[:, at(i)], vl[:, at(i)] = split(v)
    for i in range(per + 2):
        band = block(base + i)
        blurred = mm3((window(vh, i + 1), window(vl, i + 1)), (bh_ref[band, :], bl_ref[band, :]), NT)
        u = field(base + i - 1) / blurred
        if i < 1:
            u = jnp.where(base > 0, u, 0.0)
        if i >= per + 1:
            u = jnp.where(base + per < blocks, u, 0.0)
        uh[:, at(i)], ul[:, at(i)] = split(u)

    def stack(ref, j):
        half = LANES // 2
        after = ref[pl.ds(pl.multiple_of((j + 1) * LANES, LANES), half), LANES:]
        before = ref[pl.ds(pl.multiple_of((j - 1) * LANES + half, half), half), LANES:]
        return jnp.concatenate([ref[block(j), 0:LANES], after, before], axis=0)

    for i in range(per):
        bh = stack(bh_ref, base + i + 1)
        bl = stack(bl_ref, base + i + 1)
        total = mm3((window(uh, i + 1), window(ul, i + 1)), (bh, bl), NN)
        weight = jnp.sum(bh.astype(F32) + bl.astype(F32), axis=0, keepdims=True)
        out[:, block(i ^ flip)] = field(base + i) * total / weight


def smear(d, idx, field, bh, bl):
    rows, width = field.shape
    blocks = width // LANES
    per = blocks // 4
    scratch = [pltpu.VMEM((rows, (per + 4) * LANES), BF16)] * 2 + [pltpu.VMEM((rows, (per + 2) * LANES), BF16)] * 2
    return call(
        functools.partial(smear_kernel, blocks, d),
        [(rows, width // 4), (8, LANES)],
        [idx, field, bh, bl],
        "smear",
        rows * width * LANES,
        scratch,
        1,
        {2: 2, 3: 3},
    )


def fold(x):
    return jnp.sum(jnp.sum(x.reshape(4, x.shape[0] // 32, 8, x.shape[1]), axis=1), axis=0)


def numerator(x, loads, pair, tile):
    return mm_short(split(jnp.transpose(loads)), split(x / mm_short(split(loads), pair, NT)), NN)


def first_kernel(l, h, x, out, sums):
    half = h.shape[0]
    out[...] = numerator(x[:, half:], l[...], split(h[...]), half)
    sums[...] = fold(l[...])


def middle_kernel(l, h, x, before, before_sums, out, sums):
    half = h.shape[0]
    out[...] = before[...] + numerator(x[:, half:], l[...], split(h[...]), half)
    sums[...] = before_sums[...] + fold(l[...])


def last_kernel(l, h, x, before, before_sums, out):
    half = h.shape[0]
    out[0:half, :] = jnp.transpose(before[...] + numerator(x[:, half:], l[...], split(h[...]), half))
    out[half : half + 8, :] = before_sums[...] + fold(l[...])


def keep_kernel(x0, x1, x2, x3, l0, l1, l2, l3, h_ref, out):
    half = h_ref.shape[0]
    loads = jnp.concatenate([l[...] for l in (l0, l1, l2, l3)], axis=0)
    left, left_t = split(loads), split(jnp.transpose(loads))
    tile = 256
    for t in range(half // tile):
        h = split(h_ref[t * tile : (t + 1) * tile, :])
        x = jnp.concatenate([r[:, t * tile : (t + 1) * tile] for r in (x0, x1, x2, x3)], axis=0)
        quotient = split(x / mm_short(left, h, NT))
        out[t * tile : (t + 1) * tile, :] = jnp.transpose(mm3(left_t, quotient, NN))
    out[half : half + 8, :] = fold(loads)


def components_part(xs, ls, mine, theirs, order):
    half, comps = mine.shape
    rows = xs[0].shape[0]
    macs = 2 * rows * half * comps
    a, b, c, d = order
    state = call(first_kernel, [(comps, half), (8, comps)], [ls[a], theirs, xs[a]], "components_first", macs)
    state = call(middle_kernel, [(comps, half), (8, comps)], [ls[b], theirs, xs[b], *state], "components_middle", macs)
    state = call(middle_kernel, [(comps, half), (8, comps)], [ls[c], theirs, xs[c], *state], "components_middle", macs)
    send = call(last_kernel, [(half + 8, comps)], [ls[d], theirs, xs[d], *state], "components_last", macs)[0]
    keep = call(keep_kernel, [(half + 8, comps)], [*xs, *ls, mine], "components_keep", 4 * macs)[0]
    return keep, send


def own_half_kernel(x0, x1, x2, x3, l0, l1, l2, l3, h_ref, o0, o1, o2, o3):
    pair = split(h_ref[...])
    half = h_ref.shape[0]
    for x, l, out in zip((x0, x1, x2, x3), (l0, l1, l2, l3), (o0, o1, o2, o3)):
        out[...] = mm3(split(x[:, 0:half] / mm_short(split(l[...]), pair, NT)), pair, NN)


def other_half_kernel(x, l, h_ref, own, before, out):
    pair = split(h_ref[...])
    half = h_ref.shape[0]
    rows = l.shape[0]
    out[0:rows, :] = before[...] + mm3(split(x[:, half:] / mm_short(split(l[...]), pair, NT)), pair, NN)
    out[rows : rows + 8, :] = fold(h_ref[...]) + fold(own[...])


def loadings_part(xs, ls, mine, theirs):
    half, comps = mine.shape
    rows = xs[0].shape[0]
    macs = 2 * rows * half * comps
    first = call(own_half_kernel, [(rows, comps)] * 4, [*xs, *ls, mine], "loadings_own", 4 * macs)
    return [
        call(other_half_kernel, [(rows + 8, comps)], [xs[d], ls[d], theirs, mine, first[d]], "loadings_other", macs)[0]
        for d in range(4)
    ]


SPLIT = ("z", "c", "x", "y")


def swap(x, axis, distance):
    size = 2 if axis == "c" else 4
    return lax.ppermute(x, axis, [(i, i ^ distance) for i in range(size)])


def spread(x, axes, copies, zero=0.0):
    y = jnp.broadcast_to(x[None], (copies,) + x.shape) + zero
    return lax.all_to_all(y, axes, 0, 0).reshape((-1,) + x.shape[1:])


def local(measured, resolution, loadings_start, components_start):
    xi, yi, ci = lax.axis_index("x"), lax.axis_index("y"), lax.axis_index("c")
    zi = lax.axis_index("z")
    comps = components_start.shape[0]
    idx = jnp.stack([xi, ci]).astype(jnp.int32)
    bh, bl = make_bands(resolution)
    xs = [None] * 4
    for d in (2, 1, 3, 0):
        xs[d], zero, bh, bl = smear(d, idx, measured, bh, bl)
        if d:
            xs[d] = swap(xs[d], "x", d)
    start = spread(components_start.T, "y", 4, zero[0, 0])
    half = start.shape[0] // 2
    mine = lax.dynamic_slice_in_dim(start, ci * half, half)
    theirs = lax.dynamic_slice_in_dim(start, (1 - ci) * half, half)
    rows = measured.shape[0]
    ls = [lax.dynamic_slice_in_dim(loadings_start, ((xi ^ d) * 4 + yi) * rows, rows) for d in range(4)]
    group = 32
    part = half // group
    piece = lax.dynamic_slice_in_dim(mine, (zi * 4 + yi) * part, part)
    for step in range(ITERS):
        keep, send = components_part(xs, ls, mine, theirs, (0, 2, 1, 3))
        both = keep + swap(send, "c", 1)
        totals = jnp.sum(both[half:], axis=0)
        packed = jnp.concatenate(
            [both[:half].reshape(group, part, 1, comps), jnp.broadcast_to(totals, (group, 1, 1, comps))], axis=1
        )
        total = jnp.sum(lax.all_to_all(packed, ("z", "y"), 0, 0), axis=0)[:, 0]
        piece = piece * total[:part] / total[part:]
        mine = spread(piece, ("z", "y"), group)
        theirs = swap(mine, "c", 1)
        parts = loadings_part(xs, ls, mine, theirs)
        total = parts[0] + swap(parts[2], "x", 2) + swap(parts[1], "x", 1) + swap(parts[3], "x", 3)
        own = ls[0] * total[:rows] / jnp.sum(total[rows:], axis=0, keepdims=True)
        if step < ITERS - 1:
            ls = [own] + [swap(own, "x", d) for d in (1, 2, 3)]
    loadings = spread(own, ("x", "y"), 16)
    low = lax.dynamic_slice_in_dim(mine, (yi % 2) * (half // 2), half // 2)
    high = lax.dynamic_slice_in_dim(theirs, (yi % 2) * (half // 2), half // 2)
    components = jnp.where(yi // 2 == ci, low, high).T
    return (loadings, components)


def solution(mesh):
    inner = Mesh(mesh.devices.reshape(8, 2, 4, 4), SPLIT)
    return jax.shard_map(
        local,
        mesh=inner,
        in_specs=(P(SPLIT, None), P(), P(("z", "c"), None), P(None, ("x", "y"))),
        out_specs=(P(("z", "c"), None), P(None, ("x", "y"))),
        check_vma=False,
    )
```

```python
import functools
import jax
import jax.numpy as jnp
from jax import lax
from jax.experimental import pallas as pl
from jax.experimental.pallas import tpu as pltpu
from jax.sharding import Mesh, PartitionSpec as P

RADIUS = 16
TAPS = 33
ITERS = 3
LANES = 128
VMEM = pltpu.MemorySpace.VMEM
SMEM = pltpu.MemorySpace.SMEM
F32 = jnp.float32
BF16 = jnp.bfloat16
NT = ((1,), (1,))
NN = ((1,), (0,))


def split(x):
    hi = x.astype(BF16)
    return hi, (x - hi.astype(F32)).astype(BF16)


def mm(a, b, dims):
    return lax.dot_general(a, b, (dims, ((), ())), preferred_element_type=F32)


def mm3(a, b, dims):
    (ah, al), (bh, bl) = a, b
    return mm(ah, bh, dims) + (mm(al, bh, dims) + mm(ah, bl, dims))


def mm_short(a, b, dims):
    (ah, al), (bh, bl) = a, b
    axis = dims[1][0]
    wide = mm(jnp.concatenate([ah, al], axis=1), jnp.concatenate([bh, bh], axis=axis), dims)
    return wide + mm(ah, bl, dims)


def block(j):
    return pl.ds(pl.multiple_of(j * LANES, LANES), LANES)


def call(kernel, outs, ins, name, macs, scratch=(), scalars=0, aliases=None):
    cost = 1024 if name == "smear" else 1 << 20
    kept = [jax.ShapeDtypeStruct(ins[i].shape, ins[i].dtype) for i in (aliases or {})]
    result = pl.pallas_call(
        kernel,
        out_shape=[jax.ShapeDtypeStruct(o, F32) for o in outs] + kept,
        in_specs=[pl.BlockSpec(memory_space=SMEM)] * scalars + [pl.BlockSpec(memory_space=VMEM)] * (len(ins) - scalars),
        out_specs=[pl.BlockSpec(memory_space=VMEM)] * (len(outs) + len(kept)),
        scratch_shapes=list(scratch),
        input_output_aliases=aliases or {},
        compiler_params=pltpu.CompilerParams(vmem_limit_bytes=8 << 20),
        cost_estimate=pl.CostEstimate(flops=cost, bytes_accessed=cost, transcendentals=0),
        name=name,
    )(*ins)
    return result


def bands_kernel(blocks, res_ref, bh, bl, pad):
    zero = jnp.zeros((LANES, 2 * LANES), BF16)
    for ref in (bh, bl):
        ref[0:LANES, :] = zero
        ref[(blocks + 1) * LANES : (blocks + 2) * LANES, :] = zero
    for ref in pad:
        ref[...] = jnp.zeros((LANES, LANES), F32)
    row = lax.broadcasted_iota(jnp.int32, (LANES, LANES), 0)
    col = lax.broadcasted_iota(jnp.int32, (LANES, LANES), 1)
    inside = jnp.abs(row - col) <= RADIUS

    def one(j, ref):
        ref[0:TAPS, :] = res_ref[:, block(j)]
        band = pltpu.roll(jnp.transpose(ref[...]), LANES - RADIUS, 1, stride=1, stride_axis=0)
        h, l = split(jnp.where(inside, band, 0.0))
        bh[block(j + 1), 0:LANES] = h
        bl[block(j + 1), 0:LANES] = l
        h, l = split(jnp.where(inside, 0.0, band))
        bh[block(j + 1), LANES:] = h
        bl[block(j + 1), LANES:] = l

    def step(i, carry):
        for u, ref in enumerate(pad):
            one(i * len(pad) + u, ref)
        return carry

    lax.fori_loop(0, blocks // len(pad), step, 0)


def make_bands(resolution):
    blocks = resolution.shape[1] // LANES
    shape = jax.ShapeDtypeStruct(((blocks + 2) * LANES, 2 * LANES), BF16)

    def kernel(res_ref, bh, bl, p0, p1, p2, p3):
        bands_kernel(blocks, res_ref, bh, bl, (p0, p1, p2, p3))

    return pl.pallas_call(
        kernel,
        out_shape=[shape] * 2,
        in_specs=[pl.BlockSpec(memory_space=VMEM)],
        out_specs=[pl.BlockSpec(memory_space=VMEM)] * 2,
        scratch_shapes=[pltpu.VMEM((LANES, LANES), F32)] * 4,
        compiler_params=pltpu.CompilerParams(vmem_limit_bytes=8 << 20),
        cost_estimate=pl.CostEstimate(flops=1 << 20, bytes_accessed=12 << 20, transcendentals=0),
        name="bands",
    )(resolution)


def smear_kernel(blocks, d, idx_ref, field_ref, bh_ref, bl_ref, out, token, _, __, vh, vl, uh, ul):
    token[...] = jnp.zeros(token.shape, F32)
    rows = field_ref.shape[0]
    per = blocks // 4
    base = (idx_ref[0] ^ d) * per
    flip = idx_ref[1] * (per // 2)
    near = lax.broadcasted_iota(jnp.int32, (rows, LANES), 1) < LANES // 2

    def field(j):
        return field_ref[:, block(jnp.clip(j, 0, blocks - 1))]

    def at(i):
        return slice(i * LANES, (i + 1) * LANES)

    def window(ref, i):
        return jnp.concatenate([ref[:, at(i)], jnp.where(near, ref[:, at(i + 1)], ref[:, at(i - 1)])], axis=1)

    for i in range(per + 4):
        v = field(base + i - 2)
        if i < 2:
            v = jnp.where(base > 0, v, 0.0)
        if i >= per + 2:
            v = jnp.where(base + per < blocks, v, 0.0)
        vh[:, at(i)], vl[:, at(i)] = split(v)
    for i in range(per + 2):
        band = block(base + i)
        blurred = mm3((window(vh, i + 1), window(vl, i + 1)), (bh_ref[band, :], bl_ref[band, :]), NT)
        u = field(base + i - 1) / blurred
        if i < 1:
            u = jnp.where(base > 0, u, 0.0)
        if i >= per + 1:
            u = jnp.where(base + per < blocks, u, 0.0)
        uh[:, at(i)], ul[:, at(i)] = split(u)

    def stack(ref, j):
        half = LANES // 2
        after = ref[pl.ds(pl.multiple_of((j + 1) * LANES, LANES), half), LANES:]
        before = ref[pl.ds(pl.multiple_of((j - 1) * LANES + half, half), half), LANES:]
        return jnp.concatenate([ref[block(j), 0:LANES], after, before], axis=0)

    for i in range(per):
        bh = stack(bh_ref, base + i + 1)
        bl = stack(bl_ref, base + i + 1)
        total = mm3((window(uh, i + 1), window(ul, i + 1)), (bh, bl), NN)
        weight = jnp.sum(bh.astype(F32) + bl.astype(F32), axis=0, keepdims=True)
        out[:, block(i ^ flip)] = field(base + i) * total / weight


def smear(d, idx, field, bh, bl):
    rows, width = field.shape
    blocks = width // LANES
    per = blocks // 4
    scratch = [pltpu.VMEM((rows, (per + 4) * LANES), BF16)] * 2 + [pltpu.VMEM((rows, (per + 2) * LANES), BF16)] * 2
    return call(
        functools.partial(smear_kernel, blocks, d),
        [(rows, width // 4), (8, LANES)],
        [idx, field, bh, bl],
        "smear",
        rows * width * LANES,
        scratch,
        1,
        {2: 2, 3: 3},
    )


def last_smear_kernel(blocks, d, idx_ref, field_ref, res_ref, _, out, bh, bl, pad, vh, vl, uh, ul):
    rows = field_ref.shape[0]
    per = blocks // 4
    base = (idx_ref[0] ^ d) * per
    flip = idx_ref[1] * (per // 2)
    near = lax.broadcasted_iota(jnp.int32, (rows, LANES), 1) < LANES // 2
    row = lax.broadcasted_iota(jnp.int32, (LANES, LANES), 0)
    col = lax.broadcasted_iota(jnp.int32, (LANES, LANES), 1)
    inside = jnp.abs(row - col) <= RADIUS
    left, right = base > 0, base + per < blocks

    def take(ref, j):
        return ref[:, block(jnp.clip(j, 0, blocks - 1))]

    def at(i):
        return slice(i * LANES, (i + 1) * LANES)

    def valid(i, margin, x):
        if i < margin:
            return jnp.where(left, x, 0.0)
        return jnp.where(right, x, 0.0) if i >= per + margin else x

    def window(ref, i):
        return jnp.concatenate([ref[:, at(i)], jnp.where(near, ref[:, at(i + 1)], ref[:, at(i - 1)])], axis=1)

    pad[...] = jnp.zeros(pad.shape, F32)

    def bands(step, carry):
        for u in range((per + 2) // 2):
            i = step * ((per + 2) // 2) + u
            j = base + i - 1
            pad[u, 0:TAPS, :] = jnp.where((j >= 0) & (j < blocks), take(res_ref, j), 0.0)
            band = pltpu.roll(jnp.transpose(pad[u]), LANES - RADIUS, 1, stride=1, stride_axis=0)
            bh[block(i), 0:LANES], bl[block(i), 0:LANES] = split(jnp.where(inside, band, 0.0))
            bh[block(i), LANES:], bl[block(i), LANES:] = split(jnp.where(inside, 0.0, band))
        return carry

    lax.fori_loop(0, 2, bands, 0)
    for i in range(per + 4):
        vh[:, at(i)], vl[:, at(i)] = split(valid(i, 2, take(field_ref, base + i - 2)))
    for i in range(per + 2):
        blurred = mm3((window(vh, i + 1), window(vl, i + 1)), (bh[at(i), :], bl[at(i), :]), NT)
        uh[:, at(i)], ul[:, at(i)] = split(valid(i, 1, take(field_ref, base + i - 1) / blurred))

    def stack(ref, i):
        half = LANES // 2
        after = ref[(i + 1) * LANES : (i + 1) * LANES + half, LANES:]
        before = ref[(i - 1) * LANES + half : i * LANES, LANES:]
        return jnp.concatenate([ref[at(i), 0:LANES], after, before], axis=0)

    for i in range(per):
        h, l = stack(bh, i + 1), stack(bl, i + 1)
        total = mm3((window(uh, i + 1), window(ul, i + 1)), (h, l), NN)
        weight = jnp.sum(h.astype(F32) + l.astype(F32), axis=0, keepdims=True)
        out[:, block(i ^ flip)] = take(field_ref, base + i) * total / weight


def last_smear(d, idx, field, resolution, token):
    rows, width = field.shape
    blocks = width // LANES
    per = blocks // 4
    scratch = [pltpu.VMEM(((per + 2) * LANES, 2 * LANES), BF16)] * 2
    scratch += [pltpu.VMEM(((per + 2) // 2, LANES, LANES), F32)]
    scratch += [pltpu.VMEM((rows, (per + 4) * LANES), BF16)] * 2 + [pltpu.VMEM((rows, (per + 2) * LANES), BF16)] * 2
    return call(
        functools.partial(last_smear_kernel, blocks, d),
        [(rows, width // 4)],
        [idx, field, resolution, token],
        "smear",
        1024,
        scratch,
        1,
    )[0]


def fold(x):
    return jnp.sum(jnp.sum(x.reshape(4, x.shape[0] // 32, 8, x.shape[1]), axis=1), axis=0)


def numerator(x, loads, pair, tile):
    return mm_short(split(jnp.transpose(loads)), split(x / mm_short(split(loads), pair, NT)), NN)


def first_kernel(l, h, x, out, sums):
    half = h.shape[0]
    out[...] = numerator(x[:, half:], l[...], split(h[...]), half)
    sums[...] = fold(l[...])


def middle_kernel(l, h, x, before, before_sums, out, sums):
    half = h.shape[0]
    out[...] = before[...] + numerator(x[:, half:], l[...], split(h[...]), half)
    sums[...] = before_sums[...] + fold(l[...])


def last_kernel(l, h, x, before, before_sums, out):
    half = h.shape[0]
    out[0:half, :] = jnp.transpose(before[...] + numerator(x[:, half:], l[...], split(h[...]), half))
    out[half : half + 8, :] = before_sums[...] + fold(l[...])


def keep_kernel(x0, x1, x2, x3, l0, l1, l2, l3, h_ref, out):
    half = h_ref.shape[0]
    loads = jnp.concatenate([l[...] for l in (l0, l1, l2, l3)], axis=0)
    left, left_t = split(loads), split(jnp.transpose(loads))
    tile = 256
    for t in range(half // tile):
        h = split(h_ref[t * tile : (t + 1) * tile, :])
        x = jnp.concatenate([r[:, t * tile : (t + 1) * tile] for r in (x0, x1, x2, x3)], axis=0)
        quotient = split(x / mm_short(left, h, NT))
        out[t * tile : (t + 1) * tile, :] = jnp.transpose(mm3(left_t, quotient, NN))
    out[half : half + 8, :] = fold(loads)


def components_part(xs, ls, mine, theirs, order):
    half, comps = mine.shape
    rows = xs[0].shape[0]
    macs = 2 * rows * half * comps
    a, b, c, d = order
    state = call(first_kernel, [(comps, half), (8, comps)], [ls[a], theirs, xs[a]], "components_first", macs)
    state = call(middle_kernel, [(comps, half), (8, comps)], [ls[b], theirs, xs[b], *state], "components_middle", macs)
    state = call(middle_kernel, [(comps, half), (8, comps)], [ls[c], theirs, xs[c], *state], "components_middle", macs)
    send = call(last_kernel, [(half + 8, comps)], [ls[d], theirs, xs[d], *state], "components_last", macs)[0]
    keep = call(keep_kernel, [(half + 8, comps)], [*xs, *ls, mine], "components_keep", 4 * macs)[0]
    return keep, send


def own_half_kernel(x0, x1, x2, x3, l0, l1, l2, l3, h_ref, o0, o1, o2, o3):
    pair = split(h_ref[...])
    half = h_ref.shape[0]
    for x, l, out in zip((x0, x1, x2, x3), (l0, l1, l2, l3), (o0, o1, o2, o3)):
        out[...] = mm3(split(x[:, 0:half] / mm_short(split(l[...]), pair, NT)), pair, NN)


def other_half_kernel(x, l, h_ref, own, before, out):
    pair = split(h_ref[...])
    half = h_ref.shape[0]
    rows = l.shape[0]
    out[0:rows, :] = before[...] + mm3(split(x[:, half:] / mm_short(split(l[...]), pair, NT)), pair, NN)
    out[rows : rows + 8, :] = fold(h_ref[...]) + fold(own[...])


def loadings_part(xs, ls, mine, theirs):
    half, comps = mine.shape
    rows = xs[0].shape[0]
    macs = 2 * rows * half * comps
    first = call(own_half_kernel, [(rows, comps)] * 4, [*xs, *ls, mine], "loadings_own", 4 * macs)
    return [
        call(other_half_kernel, [(rows + 8, comps)], [xs[d], ls[d], theirs, mine, first[d]], "loadings_other", macs)[0]
        for d in range(4)
    ]


SPLIT = ("z", "c", "x", "y")


def swap(x, axis, distance):
    size = 2 if axis == "c" else 4
    return lax.ppermute(x, axis, [(i, i ^ distance) for i in range(size)])


def spread(x, axes, copies, zero=0.0):
    y = jnp.broadcast_to(x[None], (copies,) + x.shape) + zero
    return lax.all_to_all(y, axes, 0, 0).reshape((-1,) + x.shape[1:])


def local(measured, resolution, loadings_start, components_start):
    xi, yi, ci = lax.axis_index("x"), lax.axis_index("y"), lax.axis_index("c")
    zi = lax.axis_index("z")
    comps = components_start.shape[0]
    idx = jnp.stack([xi, ci]).astype(jnp.int32)
    xs = [None] * 4
    bh, bl = make_bands(resolution)
    for d in (2, 1, 3):
        xs[d], zero, bh, bl = smear(d, idx, measured, bh, bl)
        xs[d] = swap(xs[d], "x", d)
    xs[0] = last_smear(0, idx, measured, resolution, zero)
    start = spread(components_start.T, "y", 4, zero[0, 0])
    half = start.shape[0] // 2
    mine = lax.dynamic_slice_in_dim(start, ci * half, half)
    theirs = lax.dynamic_slice_in_dim(start, (1 - ci) * half, half)
    rows = measured.shape[0]
    ls = [lax.dynamic_slice_in_dim(loadings_start, ((xi ^ d) * 4 + yi) * rows, rows) for d in range(4)]
    group = 32
    part = half // group
    piece = lax.dynamic_slice_in_dim(mine, (zi * 4 + yi) * part, part)
    for step in range(ITERS):
        keep, send = components_part(xs, ls, mine, theirs, (0, 2, 1, 3))
        both = keep + swap(send, "c", 1)
        totals = jnp.sum(both[half:], axis=0)
        packed = jnp.concatenate(
            [both[:half].reshape(group, part, 1, comps), jnp.broadcast_to(totals, (group, 1, 1, comps))], axis=1
        )
        total = jnp.sum(lax.all_to_all(packed, ("z", "y"), 0, 0), axis=0)[:, 0]
        piece = piece * total[:part] / total[part:]
        mine = spread(piece, ("z", "y"), group)
        theirs = swap(mine, "c", 1)
        parts = loadings_part(xs, ls, mine, theirs)
        total = parts[0] + swap(parts[2], "x", 2) + swap(parts[1], "x", 1) + swap(parts[3], "x", 3)
        own = ls[0] * total[:rows] / jnp.sum(total[rows:], axis=0, keepdims=True)
        if step < ITERS - 1:
            ls = [own] + [swap(own, "x", d) for d in (1, 2, 3)]
    loadings = spread(own, ("x", "y"), 16)
    low = lax.dynamic_slice_in_dim(mine, (yi % 2) * (half // 2), half // 2)
    high = lax.dynamic_slice_in_dim(theirs, (yi % 2) * (half // 2), half // 2)
    components = jnp.where(yi // 2 == ci, low, high).T
    return (loadings, components)


def solution(mesh):
    inner = Mesh(mesh.devices.reshape(8, 2, 4, 4), SPLIT)
    return jax.shard_map(
        local,
        mesh=inner,
        in_specs=(P(SPLIT, None), P(), P(("z", "c"), None), P(None, ("x", "y"))),
        out_specs=(P(("z", "c"), None), P(None, ("x", "y"))),
        check_vma=False,
    )
```
